512 devices in a mesh: patch: 64 (over z, x, core), head: 4 (over y_hi), cfg: 2 (over y_lo).
Axes of the slice: x: 4, y: 8 (y_hi: 4, y_lo: 2; y = y_hi * 2 + y_lo), z: 8, core: 2. Of those that a mesh axis runs over, the one named last changes fastest.
Arguments:
- tokens: bfloat16 [16384, 1280], P(('cfg', 'patch')), parts along dimension 0, may hold values from -230 to 230, as said below
- norm_gain: float32 [1280], replicated, may hold values from 0.1 to 1.9
- norm_bias: float32 [1280], replicated, may hold values from -3 to 3
- w_query: bfloat16 [1280, 1024], P(None, 'head'), may hold values from -0.15625 to 0.15625
- w_key: bfloat16 [1280, 1024], P(None, 'head'), may hold values from -0.625 to 0.625
- w_value: bfloat16 [1280, 1024], P(None, 'head'), may hold values from -0.15625 to 0.15625
- w_out: bfloat16 [1024, 1280], P('head'), may hold values from -0.75 to 0.75
- stale_keys: bfloat16 [16384, 1024], P(('cfg', 'patch'), 'head'), parts along dimension 0, may hold values from -340 to 340, as said below
- stale_values: bfloat16 [16384, 1024], P(('cfg', 'patch'), 'head'), parts along dimension 0, may hold values from -6 to 6
Outputs:
- mixed: bfloat16 [16384, 1280], P(('cfg', 'patch'), 'head'), parts along dimension 0
The draws below stay inside these ranges and needn't reach their ends.
There are 2 independent parts, one for each index of `cfg`. The reference program is written for one: setup_inputs(seed, part) draws one part's arguments, and reference() takes and returns one part's arrays. A program takes and returns all parts, laid end to end along the dimension named above; an argument that names none is the same for every part. Nothing has to cross between parts.
Inputs may be any that keep to these rules, and one draw needn't show every extreme that they name: `tokens`: Real-valued activations of order one to a few tens. `stale_keys`: Real-valued keys.
All inputs are finite; a program needn't handle non-finite values.
Results may differ from the reference program's by a relative error of at most 0.015.
The reference program's roundings to bfloat16 on the way (of `normed`, `weights` and `attended`) count: a program that leaves them out, or rounds other values in their place, can miss the bound.
Values may be sent and summed in bfloat16 or wider, within the bound.
A program may use at most 64 MiB of HBM per device.

```python
import jax
import jax.numpy as jnp
from jax import lax

C = 1280
HEAD_DIM = 64
HEADS = 16
GROUPS = 32
COLS = 128
ROWS = 64
TOKENS = 8192
INNER = 1024
N_PATCH = 64


def draw_tokens(key, part):
    key = jax.random.fold_in(key, 5)
    key_body, key_chan, key_shift = jax.random.split(key, 3)
    frac = (jnp.arange(TOKENS) // COLS).astype(jnp.float32) / max(ROWS - 1, 1)
    noise = jnp.clip(jax.random.normal(key_body, (TOKENS, C), jnp.float32), -4.0, 4.0)
    row_scale = 10.0 ** frac
    chan_scale = 10.0 ** (0.5 * jax.random.uniform(key_chan, (C,), jnp.float32))
    shift = 0.5 * jnp.clip(jax.random.normal(key_shift, (C,), jnp.float32), -3.0, 3.0)
    result = row_scale[:, None] * (chan_scale[None, :] * noise + shift[None, :] * (2.0 * frac - 1.0)[:, None])
    return result.astype(jnp.bfloat16)


def draw_stale_keys(key, part):
    key = jax.random.fold_in(key, 9)
    key_base = jax.random.fold_in(key, 0)
    result = 2.5 * jnp.clip(jax.random.normal(key_base, (TOKENS, INNER), jnp.float32), -4.0, 4.0)
    return result.astype(jnp.bfloat16)


def block_levels(key, shape, shards, low, largest):
    def one(dim, parts):
        steps = jax.random.uniform(jax.random.fold_in(jax.random.fold_in(key, 6), dim), (parts,), jnp.float32, low / len(shards), largest / len(shards))
        return jnp.repeat(jnp.exp(steps), shape[dim] // parts).reshape((-1,) + (1,) * (len(shape) - dim - 1))

    factor_of = one(*shards[0])
    for cut in shards[1:]:
        factor_of = factor_of * one(*cut)
    return factor_of


def centred(key, shape, scale, most, shards=(), kind=jnp.bfloat16):
    loudness = block_levels(key, shape, shards, -0.22, 0.18) if shards else 1.0
    array = jax.random.normal(key, shape, jnp.float32) * scale * loudness
    return jnp.minimum(jnp.maximum(array, -most), most).astype(kind)


def setup_inputs(seed: int = 0, part: int = 0) -> dict:
    key_list = jax.random.split(jax.random.key(seed), 10)
    part_keys = jax.random.split(jax.random.fold_in(key_list[9], part), 10)
    return {
        "tokens": draw_tokens(jax.random.fold_in(jax.random.fold_in(key_list[9], part), 71), part),
        "norm_gain": jnp.clip(1.0 + 0.18 * jax.random.normal(key_list[1], (C,), jnp.float32), 0.1, 1.9),
        "norm_bias": centred(key_list[2], (C,), 0.5, 3.0, (), jnp.float32),
        "w_query": centred(key_list[3], (C, INNER), C ** -0.5, 0.15625, ((1, 4),)),
        "w_key": centred(key_list[4], (C, INNER), (C // 12) ** -0.5, 0.625, ((1, 4),)),
        "w_value": centred(key_list[5], (C, INNER), C ** -0.5, 0.15625, ((1, 4),)),
        "w_out": centred(key_list[6], (INNER, C), (INNER // 16) ** -0.5, 0.75, ((0, 4),)),
        "stale_keys": draw_stale_keys(jax.random.fold_in(jax.random.fold_in(key_list[9], part), 71), part),
        "stale_values": centred(part_keys[8], (TOKENS, INNER), 1.0, 6.0, ((0, 64), (1, 4))),
    }


epsilon = 1e-06

def reference(tokens, norm_gain, norm_bias, w_query, w_key, w_value, w_out, stale_keys, stale_values):
    values_in = tokens.astype(jnp.float32).reshape(TOKENS, GROUPS, C // GROUPS)
    group_mean = lax.optimization_barrier(jnp.mean(values_in, axis=(0, 2)))
    centered = values_in - group_mean[None, :, None]
    group_var = lax.optimization_barrier(jnp.mean(centered * centered, axis=(0, 2)))
    normed = (centered * lax.rsqrt(group_var + epsilon)[None, :, None]).reshape(TOKENS, C)
    normed = (normed * norm_gain + norm_bias).astype(jnp.bfloat16)
    query = jnp.dot(normed, w_query, preferred_element_type=jnp.float32).astype(jnp.bfloat16)
    fresh_keys = jnp.dot(normed, w_key, preferred_element_type=jnp.float32).astype(jnp.bfloat16)
    fresh_values = jnp.dot(normed, w_value, preferred_element_type=jnp.float32).astype(jnp.bfloat16)
    tok_dev = TOKENS // N_PATCH

    def per_block(index):
        start = index.astype(jnp.int32) * tok_dev
        queries = lax.dynamic_slice_in_dim(query, start, tok_dev, 0)
        queries = queries.reshape(tok_dev, HEADS, HEAD_DIM).astype(jnp.float32)
        own_keys = lax.dynamic_slice_in_dim(fresh_keys, start, tok_dev, 0)
        own_values = lax.dynamic_slice_in_dim(fresh_values, start, tok_dev, 0)
        keys = lax.dynamic_update_slice_in_dim(stale_keys, own_keys, start, 0)
        values = lax.dynamic_update_slice_in_dim(stale_values, own_values, start, 0)
        keys = keys.reshape(TOKENS, HEADS, HEAD_DIM).astype(jnp.float32)
        values = values.reshape(TOKENS, HEADS, HEAD_DIM).astype(jnp.float32)
        scores = jnp.einsum('qhd,khd->qhk', queries, keys) * 0.125
        top = lax.optimization_barrier(jnp.max(scores, axis=2))
        weights = jnp.exp(scores - top[..., None])
        total = lax.optimization_barrier(jnp.sum(weights, axis=2))
        rounded = lax.optimization_barrier(weights.astype(jnp.bfloat16))
        summed = jnp.einsum('qhk,khd->qhd', rounded.astype(jnp.float32), values)
        return (summed / total[..., None]).reshape(tok_dev, INNER).astype(jnp.bfloat16)
    attended = lax.map(per_block, jnp.arange(N_PATCH, dtype=jnp.int32)).reshape(TOKENS, INNER)
    return jnp.dot(attended, w_out, preferred_element_type=jnp.float32).astype(jnp.bfloat16)
```

```python
import functools

import jax
import jax.numpy as jnp
from jax import lax
from jax.experimental import pallas as pl
from jax.experimental.pallas import tpu as pltpu
from jax.sharding import PartitionSpec as P

HEAD_DIM = 64
GROUPS = 32
EPSILON = 1e-06
X = 4
CORES = 2
LANES = 128
MESH = pl.DeviceIdType.MESH
NT = (((1,), (1,)), ((), ()))
TN = (((0,), (0,)), ((), ()))
F32 = jnp.float32
BF16 = jnp.bfloat16


def three_parts(value):
    high = value.astype(BF16).astype(F32)
    rest = value - high
    middle = rest.astype(BF16).astype(F32)
    low = (rest - middle).astype(BF16).astype(F32)
    return [high, middle, low]


def stack_rows(rows, height):
    width = rows[0].shape[1]
    index = lax.broadcasted_iota(jnp.int32, (height, width), 0)
    stacked = jnp.zeros((height, width), F32)
    for i, row in enumerate(rows):
        stacked = jnp.where(index == i, row, stacked)
    return stacked.astype(BF16)


def kernel(
    n_patch,
    n_head,
    tokens,
    gain,
    bias,
    w_query,
    w_key,
    w_value,
    w_out,
    stale_keys,
    stale_values,
    out,
    tok_v,
    wq_v,
    wk_v,
    wv_v,
    wo_all,
    groups_v,
    kv,
    qbuf,
    osend,
    lsend,
    obuf,
    lbuf,
    att,
    st_send,
    st_a,
    st_b,
    ld_sem,
    wo_ld_sem,
    kv_ld_sem,
    sta_send,
    sta_recv,
    stb_send,
    stb_recv,
    kv_send,
    kv_recv,
    q_send,
    q_recv,
    o_send,
    o_recv,
    l_send,
    l_recv,
    wo_send,
    wo_recv,
    wf_send,
    wf_recv,
    att_send,
    att_recv,
):
    n_z = n_patch // (X * CORES)
    plane = X * CORES
    rows, channels = tok_v.shape
    per_group = channels // GROUPS
    own_stale = 2 * n_z
    me = lax.axis_index("patch")
    head = lax.axis_index("head")
    z = me // plane
    x = (me // CORES) % X
    core = me % CORES
    columns = channels // n_head
    wide = wo_all.shape[3]

    def at(zz, xx, cc):
        return {"patch": (zz * X + xx) * CORES + cc}

    def z_peer(k):
        return at((z + k) % n_z, x, core)

    def x_peer(k):
        return at(z, (x + k) % X, core)

    def plane_peer(k):
        rank = (x * CORES + core + k) % plane
        return {"patch": z * plane + rank}

    def head_peer(k):
        return {"head": (head + k) % n_head}

    sibling = at(z, x, 1 - core)

    def remote(src, dst, send, recv, device):
        return pltpu.make_async_remote_copy(
            src_ref=src, dst_ref=dst, send_sem=send, recv_sem=recv, device_id=device, device_id_type=MESH
        )

    barrier = pltpu.get_barrier_semaphore()
    peers = [plane_peer(k) for k in range(1, plane)]
    peers += [z_peer(k) for k in range(1, n_z)]
    peers += [head_peer(k) for k in range(1, n_head)]
    for peer in peers:
        pl.semaphore_signal(barrier, inc=1, device_id=peer, device_id_type=MESH)

    load_tok = pltpu.make_async_copy(tokens, tok_v, ld_sem.at[0])
    load_tok.start()
    load_kv = []
    for p in range(2):
        for which, source in enumerate((stale_keys, stale_values)):
            copy = pltpu.make_async_copy(
                source.at[:, p * LANES : (p + 1) * LANES], kv.at[p, own_stale, which], kv_ld_sem.at[p, which]
            )
            copy.start()
            load_kv.append(copy)
    load_w = [
        pltpu.make_async_copy(source, target, ld_sem.at[1 + i])
        for i, (source, target) in enumerate(((w_query, wq_v), (w_key, wk_v), (w_value, wv_v)))
    ]
    for copy in load_w:
        copy.start()

    def first_column(h):
        return pl.multiple_of((h * columns) // LANES * LANES, LANES)

    load_wo = [
        pltpu.make_async_copy(
            w_out.at[p * LANES : (p + 1) * LANES, pl.ds(first_column(head), wide)], wo_all.at[0, p], wo_ld_sem.at[p]
        )
        for p in range(2)
    ]
    for copy in load_wo:
        copy.start()

    channel = lax.broadcasted_iota(jnp.int32, (channels, LANES), 0)
    first = lax.broadcasted_iota(jnp.int32, (channels, LANES), 1) * per_group
    groups_v[...] = ((channel >= first) & (channel < first + per_group)).astype(F32).astype(BF16)

    def to_groups(row):
        parts = jnp.dot(stack_rows(three_parts(row), 16), groups_v[...], preferred_element_type=F32)
        return jnp.sum(parts, axis=0, keepdims=True)

    def to_channels(*values):
        stacked = stack_rows([part for value in values for part in three_parts(value)], 16)
        spread = lax.dot_general(stacked, groups_v[...], NT, preferred_element_type=F32)
        return [
            spread[3 * i : 3 * i + 1] + spread[3 * i + 1 : 3 * i + 2] + spread[3 * i + 2 : 3 * i + 3]
            for i in range(len(values))
        ]

    load_tok.wait()
    own_count = rows * per_group
    own_mean = to_groups(jnp.sum(tok_v[...].astype(F32), axis=0, keepdims=True)) * (1.0 / own_count)
    (shift,) = to_channels(own_mean)
    centred = tok_v[...].astype(F32) - shift
    own_squares = to_groups(jnp.sum(centred * centred, axis=0, keepdims=True))

    index8 = lax.broadcasted_iota(jnp.int32, (8, LANES), 0)

    def packet(mean, squares):
        return jnp.where(index8 == 0, mean, jnp.where(index8 == 1, squares, 0.0))

    def join(stats, count):
        shares = stats.shape[0]
        total = jnp.sum(stats, axis=0)
        mean = total * (1.0 / shares)
        apart = stats - mean[None]
        spread = jnp.sum(apart * apart, axis=0)
        return mean[0:1], total[1:2] + count * spread[0:1]

    own_packet = packet(own_mean, own_squares)
    st_send[0] = own_packet
    st_a[0] = own_packet

    pl.semaphore_wait(barrier, len(peers))

    stat_a = [
        remote(st_send.at[0], st_a.at[k], sta_send.at[k], sta_recv.at[k], plane_peer(k)) for k in range(1, plane)
    ]
    for copy in stat_a:
        copy.start()

    up = n_z // 2

    def kv_copy(p, src, dst, device):
        return remote(kv.at[p, src], kv.at[p, dst], kv_send.at[p, dst], kv_recv.at[p, dst], device)

    def kv_arrived(p, slot):
        kv_copy(p, own_stale, slot, sibling).wait_recv()

    def kv_first(p):
        load_kv[2 * p].wait()
        load_kv[2 * p + 1].wait()
        kv_copy(p, own_stale, 1, z_peer(1)).start()
        kv_copy(p, own_stale, up + 1, z_peer(n_z - 1)).start()
        kv_copy(p, own_stale, n_z, sibling).start()

    def kv_forward(p, step):
        kv_arrived(p, step)
        if step < up:
            kv_copy(p, step, step + 1, z_peer(1)).start()
        kv_copy(p, step, n_z + step, sibling).start()
        down = up + step
        if down < n_z:
            kv_arrived(p, down)
            if down + 1 < n_z:
                kv_copy(p, down, down + 1, z_peer(n_z - 1)).start()
            kv_copy(p, down, n_z + down, sibling).start()

    def kv_rest(p):
        for slot in range(n_z, 2 * n_z):
            kv_arrived(p, slot)

    kv_first(0)

    def wo_copy(k):
        return remote(
            w_out.at[pl.ds(core * LANES, LANES), pl.ds(first_column((head + k) % n_head), wide)],
            wo_all.at[n_head - k, core],
            wo_send.at[n_head - k],
            wo_recv.at[n_head - k],
            head_peer(k),
        )

    def wo_forward(s):
        return remote(wo_all.at[s, core], wo_all.at[s, core], wf_send.at[s], wf_recv.at[s], sibling)

    def wo_from_sibling(s):
        return remote(wo_all.at[s, core], wo_all.at[s, 1 - core], wf_send.at[s], wf_recv.at[s], sibling)

    for k in range(1, n_head):
        wo_copy(k).start()

    for copy in stat_a:
        copy.wait_recv()
    mean, squares = join(st_a[...], own_count)
    plane_packet = packet(mean, squares)
    st_send[1] = plane_packet
    st_b[0] = plane_packet
    stat_b = [remote(st_send.at[1], st_b.at[k], stb_send.at[k], stb_recv.at[k], z_peer(k)) for k in range(1, n_z)]
    for copy in stat_b:
        copy.start()

    kv_forward(0, 1)
    kv_first(1)

    for copy in stat_b:
        copy.wait_recv()
    mean, squares = join(st_b[...], own_count * plane)
    inverse = lax.rsqrt(squares * (1.0 / (own_count * n_patch)) + EPSILON)
    mean_of, inverse_of = to_channels(mean, inverse)
    normed = (tok_v[...].astype(F32) - mean_of) * inverse_of
    normed = (normed * gain[...].reshape(1, channels) + bias[...].reshape(1, channels)).astype(BF16)

    load_w[0].wait()
    query = jnp.dot(normed, wq_v[...], preferred_element_type=F32).astype(BF16) * jnp.asarray(0.125, BF16)
    q_copies = []
    for p in range(2):
        qbuf[0, p] = query[:, p * LANES : (p + 1) * LANES]

    def q_copy(p, k):
        return remote(
            qbuf.at[0, p], qbuf.at[X - k, p], q_send.at[X - k, p], q_recv.at[X - k, p], x_peer(k)
        )

    for p in range(2):
        for k in range(1, X):
            q_copy(p, k).start()

    kv_forward(0, 2)

    load_w[1].wait()
    fresh = jnp.dot(normed, wk_v[...], preferred_element_type=F32).astype(BF16)
    for p in range(2):
        kv[p, 0, 0] = fresh[:, p * LANES : (p + 1) * LANES]
    load_w[2].wait()
    fresh = jnp.dot(normed, wv_v[...], preferred_element_type=F32).astype(BF16)
    for p in range(2):
        kv[p, 0, 1] = fresh[:, p * LANES : (p + 1) * LANES]

    kv_forward(0, 3)
    kv_forward(1, 1)
    kv_forward(0, 4)
    kv_rest(0)

    lane = lax.broadcasted_iota(jnp.int32, (rows, LANES), 1)
    first_half = lane < HEAD_DIM
    blocks = 2
    ones = jnp.ones((blocks * rows, LANES), BF16)

    def o_copy(p, j):
        return remote(osend.at[p, j], obuf.at[p, X - j], o_send.at[p, j], o_recv.at[p, X - j], x_peer(j))

    def l_copy(p, j):
        return remote(lsend.at[p, j], lbuf.at[p, X - j], l_send.at[p, j], l_recv.at[p, X - j], x_peer(j))

    def attend(p, j):
        @pl.when(j != 0)
        def _():
            remote(qbuf.at[0, p], qbuf.at[j, p], q_send.at[j, p], q_recv.at[j, p], sibling).wait_recv()

        start = jnp.where(j == 0, 0, 1)
        q = qbuf[j, p]
        q_of = [jnp.where(first_half == (h == 0), q, jnp.zeros_like(q)) for h in range(2)]
        top, summed = [None, None], [None, None]
        for c in range(2 * n_z // blocks):
            keys = kv[p, pl.ds(start + blocks * c, blocks), 0].reshape(blocks * rows, LANES)
            values = kv[p, pl.ds(start + blocks * c, blocks), 1].reshape(blocks * rows, LANES)
            values = jnp.concatenate([values, ones], axis=1)
            for h in range(2):
                scores = lax.dot_general(q_of[h], keys, NT, preferred_element_type=F32)
                new_top = jnp.max(scores, axis=1, keepdims=True)
                if c:
                    new_top = jnp.maximum(top[h], new_top)
                weights = jnp.exp(scores - new_top).astype(BF16)
                more = jnp.dot(weights, values, preferred_element_type=F32)
                summed[h] = summed[h] * jnp.exp(top[h] - new_top) + more if c else more
                top[h] = new_top
        total = [summed[h][:, LANES:] for h in range(2)]
        osend[p, j] = jnp.where(
            first_half, summed[0][:, :LANES] / total[0], summed[1][:, :LANES] / total[1]
        ).astype(BF16)
        logs = jnp.where(lane == 0, top[0] + jnp.log(total[0]), top[1] + jnp.log(total[1]))
        lsend[p, j] = jnp.transpose(logs)[:8]

        @pl.when(j != 0)
        def _():
            o_copy(p, j).start()
            l_copy(p, j).start()

    def att_copy(p, k):
        return remote(
            att.at[0, p], att.at[n_head - k, p], att_send.at[n_head - k, p], att_recv.at[n_head - k, p], head_peer(k)
        )

    def combine(p):
        for s in range(1, X):
            o_copy(p, X - s).wait_recv()
            l_copy(p, X - s).wait_recv()
        logs = [lsend[p, 0]] + [lbuf[p, s] for s in range(1, X)]
        top = functools.reduce(jnp.maximum, logs)
        share = [jnp.exp(value - top) for value in logs]
        inverse_total = 1.0 / functools.reduce(jnp.add, share)
        parts = []
        for value in share:
            three = three_parts(value * inverse_total)
            parts.append(stack_rows([part[h : h + 1] for part in three for h in range(2)], 16))
        of_head = lax.broadcasted_iota(jnp.int32, (16, LANES), 0) % 2
        in_head = lax.broadcasted_iota(jnp.int32, (16, LANES), 1) // HEAD_DIM
        spread = (of_head == in_head).astype(F32).astype(BF16)
        joined = None
        for s in range(X):
            partial = osend[p, 0] if s == 0 else obuf[p, s]
            weight = lax.dot_general(parts[s], spread, TN, preferred_element_type=F32)
            term = weight * partial.astype(F32)
            joined = term if joined is None else joined + term
        att[0, p] = joined.astype(BF16)
        for k in range(1, n_head):
            att_copy(p, k).start()

    def first_pair(i, carry):
        attend(0, i)

        @pl.when(i == 0)
        def _():
            kv_forward(1, 2)

        @pl.when(i == 1)
        def _():
            kv_forward(1, 3)

        @pl.when(i == 2)
        def _():
            kv_forward(1, 4)

        return carry

    lax.fori_loop(0, X, first_pair, 0)
    kv_rest(1)
    for s in range(1, n_head):
        wo_copy(n_head - s).wait_recv()
        wo_forward(s).start()

    def second_pair(i, carry):
        attend(1, (i + 1) % X)

        @pl.when(i == 0)
        def _():
            combine(0)

        return carry

    lax.fori_loop(0, X, second_pair, 0)
    combine(1)

    for copy in load_wo:
        copy.wait()
    for s in range(1, n_head):
        wo_from_sibling(s).wait_recv()
    mixed = None
    for p in range(2):
        for s in range(n_head):
            if s:
                att_copy(p, n_head - s).wait_recv()
            term = jnp.dot(att[s, p], wo_all[s, p], preferred_element_type=F32)
            mixed = term if mixed is None else mixed + term
    shift = (head * columns) % LANES
    rolled = pltpu.roll(mixed, wide - LANES // 2, 1)
    mixed = jnp.where(shift == 0, mixed, rolled)
    out[...] = mixed[:, :columns].astype(BF16)

    for copy in stat_a + stat_b:
        copy.wait_send()
    for p in range(2):
        for slot in range(1, 2 * n_z):
            kv_copy(p, own_stale, slot, sibling).wait_send()
        for k in range(1, X):
            q_copy(p, k).wait_send()
            o_copy(p, k).wait_send()
            l_copy(p, k).wait_send()
        for k in range(1, n_head):
            att_copy(p, k).wait_send()
    for k in range(1, n_head):
        wo_copy(k).wait_send()
        wo_forward(k).wait_send()


def per_device(n_patch, n_head, *operands):
    tokens, _, _, w_query = operands[:4]
    rows, channels = tokens.shape
    inner = w_query.shape[1]
    n_z = n_patch // (X * CORES)
    columns = channels // n_head
    wide = -(-(columns + LANES // 2) // LANES) * LANES
    pairs = inner // LANES
    dma = pltpu.SemaphoreType.DMA
    any_space = pl.BlockSpec(memory_space=pl.ANY)
    vmem_space = pl.BlockSpec(memory_space=pltpu.VMEM)
    return pl.pallas_call(
        functools.partial(kernel, n_patch, n_head),
        out_shape=jax.ShapeDtypeStruct((rows, columns), BF16),
        in_specs=[any_space, vmem_space, vmem_space] + [any_space] * 6,
        out_specs=vmem_space,
        scratch_shapes=[
            pltpu.VMEM((rows, channels), BF16),
            pltpu.VMEM((channels, inner), BF16),
            pltpu.VMEM((channels, inner), BF16),
            pltpu.VMEM((channels, inner), BF16),
            pltpu.VMEM((n_head, pairs, LANES, wide), BF16),
            pltpu.VMEM((channels, LANES), BF16),
            pltpu.VMEM((pairs, 2 * n_z + 1, 2, rows, LANES), BF16),
            pltpu.VMEM((X, pairs, rows, LANES), BF16),
            pltpu.VMEM((pairs, X, rows, LANES), BF16),
            pltpu.VMEM((pairs, X, 8, LANES), F32),
            pltpu.VMEM((pairs, X, rows, LANES), BF16),
            pltpu.VMEM((pairs, X, 8, LANES), F32),
            pltpu.VMEM((n_head, pairs, rows, LANES), BF16),
            pltpu.VMEM((2, 8, LANES), F32),
            pltpu.VMEM((X * CORES, 8, LANES), F32),
            pltpu.VMEM((n_z, 8, LANES), F32),
            dma((4,)),
            dma((2,)),
            dma((2, 2)),
            dma((X * CORES,)),
            dma((X * CORES,)),
            dma((n_z,)),
            dma((n_z,)),
            dma((2, 2 * n_z)),
            dma((2, 2 * n_z)),
            dma((X, 2)),
            dma((X, 2)),
            dma((2, X)),
            dma((2, X)),
            dma((2, X)),
            dma((2, X)),
            dma((n_head,)),
            dma((n_head,)),
            dma((n_head,)),
            dma((n_head,)),
            dma((n_head, 2)),
            dma((n_head, 2)),
        ],
        compiler_params=pltpu.CompilerParams(
            collective_id=0, has_side_effects=True, vmem_limit_bytes=32 * 1024 * 1024
        ),
    )(*operands)


def solution(mesh):
    in_specs = (
        P(("cfg", "patch"), None),
        P(),
        P(),
        P(None, "head"),
        P(None, "head"),
        P(None, "head"),
        P("head", None),
        P(("cfg", "patch"), "head"),
        P(("cfg", "patch"), "head"),
    )
    return jax.shard_map(
        functools.partial(per_device, mesh.shape["patch"], mesh.shape["head"]),
        mesh=mesh,
        in_specs=in_specs,
        out_specs=P(("cfg", "patch"), "head"),
        check_vma=False,
    )
```

```python
import functools

import jax
import jax.numpy as jnp
from jax import lax
from jax.experimental import pallas as pl
from jax.experimental.pallas import tpu as pltpu
from jax.sharding import PartitionSpec as P

HEAD_DIM = 64
GROUPS = 32
EPSILON = 1e-06
X = 4
CORES = 2
LANES = 128
MESH = pl.DeviceIdType.MESH
NT = (((1,), (1,)), ((), ()))
F32 = jnp.float32
BF16 = jnp.bfloat16


def three_parts(value):
    high = value.astype(BF16).astype(F32)
    rest = value - high
    middle = rest.astype(BF16).astype(F32)
    low = (rest - middle).astype(BF16).astype(F32)
    return [high, middle, low]


def stack_rows(rows, height):
    width = rows[0].shape[1]
    index = lax.broadcasted_iota(jnp.int32, (height, width), 0)
    stacked = jnp.zeros((height, width), F32)
    for i, row in enumerate(rows):
        stacked = jnp.where(index == i, row, stacked)
    return stacked.astype(BF16)


def kernel(
    n_patch,
    n_head,
    tokens,
    gain,
    bias,
    w_query,
    w_key,
    w_value,
    w_out,
    stale_keys,
    stale_values,
    out,
    gain_v,
    bias_v,
    tok_v,
    stv_v,
    wq_v,
    wk_v,
    wv_v,
    wo_all,
    wo_t,
    groups_v,
    kv,
    qbuf,
    osend,
    obuf,
    att,
    scores_a,
    scores_b,
    st_send,
    st_a,
    st_b,
    ld_sem,
    wo_ld_sem,
    sta_send,
    sta_recv,
    stb_send,
    stb_recv,
    kv_send,
    kv_recv,
    q_send,
    q_recv,
    o_send,
    o_recv,
    wo_send,
    wo_recv,
    wf_send,
    wf_recv,
    att_send,
    att_recv,
):
    n_z = n_patch // (X * CORES)
    plane = X * CORES
    rows, channels = tok_v.shape
    per_group = channels // GROUPS
    own_stale = 2 * n_z
    me = lax.axis_index("patch")
    head = lax.axis_index("head")
    z = me // plane
    x = (me // CORES) % X
    core = me % CORES
    columns = channels // n_head
    wide = wo_all.shape[3]

    def at(zz, xx, cc):
        return {"patch": (zz * X + xx) * CORES + cc}

    def z_peer(k):
        return at((z + k) % n_z, x, core)

    def x_peer(k):
        return at(z, (x + k) % X, core)

    def plane_peer(k):
        rank = (x * CORES + core + k) % plane
        return {"patch": z * plane + rank}

    def head_peer(k):
        return {"head": (head + k) % n_head}

    sibling = at(z, x, 1 - core)

    def remote(src, dst, send, recv, device):
        return pltpu.make_async_remote_copy(
            src_ref=src, dst_ref=dst, send_sem=send, recv_sem=recv, device_id=device, device_id_type=MESH
        )

    barrier = pltpu.get_barrier_semaphore()
    peers = [plane_peer(k) for k in range(1, plane)]
    peers += [z_peer(k) for k in range(1, n_z)]
    peers += [head_peer(k) for k in range(1, n_head)]
    for peer in peers:
        pl.semaphore_signal(barrier, inc=1, device_id=peer, device_id_type=MESH)

    def load(source, target, sem):
        copy = pltpu.make_async_copy(source, target, sem)
        copy.start()
        return copy

    load_tok = load(tokens, tok_v, ld_sem.at[0])
    load_stale = [
        load(stale_keys.at[:, p * LANES : (p + 1) * LANES], kv.at[p, own_stale, 0], ld_sem.at[1 + p]) for p in range(2)
    ]
    load_stale.append(load(stale_values, stv_v, ld_sem.at[3]))
    load_norm = [load(gain, gain_v, ld_sem.at[4]), load(bias, bias_v, ld_sem.at[5])]
    load_w = [
        load(source, target, ld_sem.at[6 + i])
        for i, (source, target) in enumerate(((w_query, wq_v), (w_key, wk_v), (w_value, wv_v)))
    ]

    def first_column(h):
        return pl.multiple_of((h * columns) // LANES * LANES, LANES)

    load_wo = [
        load(
            w_out.at[p * LANES : (p + 1) * LANES, pl.ds(first_column(head), wide)], wo_all.at[0, p], wo_ld_sem.at[p]
        )
        for p in range(2)
    ]

    channel = lax.broadcasted_iota(jnp.int32, (channels, LANES), 0)
    first = lax.broadcasted_iota(jnp.int32, (channels, LANES), 1) * per_group
    groups_v[...] = ((channel >= first) & (channel < first + per_group)).astype(F32).astype(BF16)

    def to_groups(row):
        parts = jnp.dot(stack_rows(three_parts(row), 16), groups_v[...], preferred_element_type=F32)
        return jnp.sum(parts, axis=0, keepdims=True)

    def to_channels(*values):
        stacked = stack_rows([part for value in values for part in three_parts(value)], 16)
        spread = lax.dot_general(stacked, groups_v[...], NT, preferred_element_type=F32)
        return [
            spread[3 * i : 3 * i + 1] + spread[3 * i + 1 : 3 * i + 2] + spread[3 * i + 2 : 3 * i + 3]
            for i in range(len(values))
        ]

    load_tok.wait()
    own_count = rows * per_group
    own_mean = to_groups(jnp.sum(tok_v[...].astype(F32), axis=0, keepdims=True)) * (1.0 / own_count)
    (shift,) = to_channels(own_mean)
    centred = tok_v[...].astype(F32) - shift
    own_squares = to_groups(jnp.sum(centred * centred, axis=0, keepdims=True))

    index8 = lax.broadcasted_iota(jnp.int32, (8, LANES), 0)

    def packet(mean, squares):
        return jnp.where(index8 == 0, mean, jnp.where(index8 == 1, squares, 0.0))

    def join(stats, count):
        shares = stats.shape[0]
        total = jnp.sum(stats, axis=0)
        mean = total * (1.0 / shares)
        apart = stats - mean[None]
        spread = jnp.sum(apart * apart, axis=0)
        return mean[0:1], total[1:2] + count * spread[0:1]

    own_packet = packet(own_mean, own_squares)
    st_send[0] = own_packet
    st_a[0] = own_packet
    for copy in load_stale:
        copy.wait()
    for p in range(2):
        kv[p, own_stale, 1] = jnp.transpose(stv_v[:, p * LANES : (p + 1) * LANES])

    pl.semaphore_wait(barrier, len(peers))

    stat_a = [
        remote(st_send.at[0], st_a.at[k], sta_send.at[k], sta_recv.at[k], plane_peer(k)) for k in range(1, plane)
    ]
    for copy in stat_a:
        copy.start()

    hops = n_z // 2

    def kv_copy(p, src, dst, device):
        return remote(kv.at[p, src], kv.at[p, dst], kv_send.at[p, dst], kv_recv.at[p, dst], device)

    def kv_arrived(p, slot):
        kv_copy(p, own_stale, slot, sibling).wait_recv()

    def kv_first(p):
        kv_copy(p, own_stale, 2, z_peer(1)).start()
        kv_copy(p, own_stale, 3, z_peer(n_z - 1)).start()
        kv_copy(p, own_stale, 1, sibling).start()

    def kv_forward(p, hop):
        slot = 4 * hop - 2
        kv_arrived(p, slot)
        if hop == hops:
            kv_copy(p, slot, slot + 1, sibling).start()
            return
        kv_copy(p, slot, slot + 4, z_peer(1)).start()
        kv_copy(p, slot, slot + 2, sibling).start()
        kv_arrived(p, slot + 1)
        if hop + 1 < hops:
            kv_copy(p, slot + 1, slot + 5, z_peer(n_z - 1)).start()
        kv_copy(p, slot + 1, slot + 3, sibling).start()

    for p in range(2):
        kv_first(p)

    def wo_copy(k):
        return remote(
            w_out.at[pl.ds(core * LANES, LANES), pl.ds(first_column((head + k) % n_head), wide)],
            wo_all.at[n_head - k, core],
            wo_send.at[n_head - k],
            wo_recv.at[n_head - k],
            head_peer(k),
        )

    def wo_forward(s):
        return remote(wo_all.at[s, core], wo_all.at[s, core], wf_send.at[s], wf_recv.at[s], sibling)

    def wo_from_sibling(s):
        return remote(wo_all.at[s, core], wo_all.at[s, 1 - core], wf_send.at[s], wf_recv.at[s], sibling)

    for k in range(1, n_head):
        wo_copy(k).start()

    for copy in stat_a:
        copy.wait_recv()
    mean, squares = join(st_a[...], own_count)
    plane_packet = packet(mean, squares)
    st_send[1] = plane_packet
    st_b[0] = plane_packet
    stat_b = [remote(st_send.at[1], st_b.at[k], stb_send.at[k], stb_recv.at[k], z_peer(k)) for k in range(1, n_z)]
    for copy in stat_b:
        copy.start()

    kv_forward(0, 1)
    kv_forward(1, 1)
    for copy in load_norm + load_w:
        copy.wait()
    kv_forward(0, 2)

    for copy in stat_b:
        copy.wait_recv()
    mean, squares = join(st_b[...], own_count * plane)
    inverse = lax.rsqrt(squares * (1.0 / (own_count * n_patch)) + EPSILON)
    mean_of, inverse_of = to_channels(mean, inverse)
    normed = (tok_v[...].astype(F32) - mean_of) * inverse_of
    normed = (normed * gain_v[...].reshape(1, channels) + bias_v[...].reshape(1, channels)).astype(BF16)

    query = jnp.dot(normed, wq_v[...], preferred_element_type=F32).astype(BF16) * jnp.asarray(0.125, BF16)
    for p in range(2):
        qbuf[0, p] = query[:, p * LANES : (p + 1) * LANES]

    def q_copy(p, k):
        return remote(qbuf.at[0, p], qbuf.at[X - k, p], q_send.at[X - k, p], q_recv.at[X - k, p], x_peer(k))

    for p in range(2):
        for k in range(1, X):
            q_copy(p, k).start()

    kv_forward(1, 2)

    fresh = jnp.dot(normed, wk_v[...], preferred_element_type=F32).astype(BF16)
    for p in range(2):
        kv[p, 0, 0] = fresh[:, p * LANES : (p + 1) * LANES]
    fresh = jnp.dot(normed, wv_v[...], preferred_element_type=F32)
    for p in range(2):
        kv[p, 0, 1] = jnp.transpose(fresh[:, p * LANES : (p + 1) * LANES]).astype(BF16)

    kv_forward(0, 3)
    kv_forward(1, 3)

    lane = lax.broadcasted_iota(jnp.int32, (rows, LANES), 1)
    blocks = 2
    span = blocks * rows
    chunks = 2 * n_z // blocks
    both = 2 * LANES

    def masked_queries(p, j):
        q = qbuf[j, p]
        return jnp.concatenate(
            [jnp.where((lane < HEAD_DIM) == (h == 0), q, jnp.zeros_like(q)) for h in range(2)], axis=0
        )

    def score_chunk(p, j, queries, c, scores_ref):
        start = (0 if j == 0 else 1) + blocks * c
        keys = kv[p, start : start + blocks, 0].reshape(span, LANES)
        scores = lax.dot_general(keys, queries, NT, preferred_element_type=F32)
        scores_ref[c * span : (c + 1) * span] = scores
        return jnp.max(scores.reshape(span // 8, 8, both), axis=0)

    def sum_chunk(p, j, top, c, scores_ref):
        start = (0 if j == 0 else 1) + blocks * c
        weights = jnp.exp(scores_ref[c * span : (c + 1) * span] - top)
        total = jnp.sum(weights.reshape(span // 8, 8, both), axis=0)
        values = jnp.concatenate([kv[p, start + i, 1] for i in range(blocks)], axis=1)
        return total, jnp.dot(values, weights.astype(BF16), preferred_element_type=F32)

    def o_copy(p, j):
        return remote(osend.at[p, j], obuf.at[p, X - j], o_send.at[p, j], o_recv.at[p, X - j], x_peer(j))

    def q_arrived(p, j):
        remote(qbuf.at[0, p], qbuf.at[j, p], q_send.at[j, p], q_recv.at[j, p], sibling).wait_recv()

    def finish(p, j, top, total, summed):
        total = jnp.sum(total, axis=0, keepdims=True)
        summed = summed * (1.0 / total)
        logs = top + jnp.log(total)
        osend[p, j, :rows] = jnp.concatenate(
            [summed[:HEAD_DIM, :LANES], summed[HEAD_DIM:, LANES:]], axis=0
        ).astype(BF16)
        three = three_parts(logs)
        osend[p, j, rows:] = stack_rows(
            [part[:, h * LANES : (h + 1) * LANES] for part in three for h in range(2)], 16
        )
        if j:
            o_copy(p, j).start()

    def att_copy(p, k):
        own = att.at[p, 0:rows]
        there = att.at[p, (n_head - k) * rows : (n_head - k + 1) * rows]
        return remote(own, there, att_send.at[n_head - k, p], att_recv.at[n_head - k, p], head_peer(k))

    def combine(p):
        for s in range(1, X):
            o_copy(p, X - s).wait_recv()
        partials = [osend[p, 0]] + [obuf[p, s] for s in range(1, X)]
        logs = []
        for partial in partials:
            parts = partial[rows:].astype(F32)
            logs.append([parts[h : h + 1] + parts[2 + h : 3 + h] + parts[4 + h : 5 + h] for h in range(2)])
        joined = []
        for h in range(2):
            top = functools.reduce(jnp.maximum, [value[h] for value in logs])
            share = [jnp.exp(value[h] - top) for value in logs]
            inverse_total = 1.0 / functools.reduce(jnp.add, share)
            terms = [
                partial[h * HEAD_DIM : (h + 1) * HEAD_DIM].astype(F32) * (value * inverse_total)
                for partial, value in zip(partials, share)
            ]
            joined.append(functools.reduce(jnp.add, terms))
        att[p, 0:rows] = jnp.concatenate(joined, axis=0).astype(BF16)
        for k in range(1, n_head):
            att_copy(p, k).start()

    units = [(0, 0)] + [(0, j) for j in range(1, X)] + [(1, j) for j in range(1, X)] + [(1, 0)]
    buffers = (scores_a, scores_b)

    queries = masked_queries(0, 0)
    top = None
    for c in range(chunks):
        if c == chunks - 1:
            kv_forward(0, hops)
            kv_forward(1, hops)
        for slot in range(blocks * c, blocks * (c + 1)):
            if slot and (slot == 1 or (slot - 2) % 4 >= 2 or slot == 2 * n_z - 1):
                kv_arrived(0, slot)
        more = score_chunk(0, 0, queries, c, scores_a)
        top = more if top is None else jnp.maximum(top, more)
    top = jnp.max(top, axis=0, keepdims=True)
    for i, (p, j) in enumerate(units):
        after = units[i + 1] if i + 1 < len(units) else None
        if after:
            if after[1]:
                q_arrived(*after)
            if after == (1, 1):
                for slot in range(1, 2 * n_z):
                    if slot == 1 or (slot - 2) % 4 >= 2 or slot == 2 * n_z - 1:
                        kv_arrived(1, slot)
            queries = masked_queries(*after)
        next_top, total, summed = None, None, None
        for c in range(chunks):
            if after:
                more = score_chunk(*after, queries, c, buffers[(i + 1) % 2])
                next_top = more if next_top is None else jnp.maximum(next_top, more)
            more, term = sum_chunk(p, j, top, c, buffers[i % 2])
            total = more if total is None else total + more
            summed = term if summed is None else summed + term
        finish(p, j, top, total, summed)
        if after:
            top = jnp.max(next_top, axis=0, keepdims=True)
        if i == 0:
            for s in range(1, n_head):
                wo_copy(n_head - s).wait_recv()
                wo_forward(s).start()
        if i == len(units) - 2:
            combine(0)

    for copy in load_wo:
        copy.wait()
    for s in range(1, n_head):
        wo_from_sibling(s).wait_recv()
    for p in range(2):
        for s in range(n_head):
            wo_t[p, :, s * LANES : (s + 1) * LANES] = jnp.transpose(wo_all[s, p])
    combine(1)

    mixed = None
    for p in range(2):
        for s in range(1, n_head):
            att_copy(p, n_head - s).wait_recv()
        term = jnp.dot(wo_t[p], att[p], preferred_element_type=F32)
        mixed = term if mixed is None else mixed + term
    shift = (head * columns) % LANES
    half = LANES // 2
    out[...] = jnp.where(shift == 0, mixed[:columns], mixed[half : half + columns]).astype(BF16)

    for copy in stat_a + stat_b:
        copy.wait_send()
    for p in range(2):
        for slot in range(1, 2 * n_z):
            kv_copy(p, own_stale, slot, sibling).wait_send()
        for k in range(1, X):
            q_copy(p, k).wait_send()
            o_copy(p, k).wait_send()
        for k in range(1, n_head):
            att_copy(p, k).wait_send()
    for k in range(1, n_head):
        wo_copy(k).wait_send()
        wo_forward(k).wait_send()


def per_device(n_patch, n_head, *operands):
    tokens, _, _, w_query = operands[:4]
    rows, channels = tokens.shape
    inner = w_query.shape[1]
    n_z = n_patch // (X * CORES)
    columns = channels // n_head
    wide = -(-(columns + LANES // 2) // LANES) * LANES
    pairs = inner // LANES
    dma = pltpu.SemaphoreType.DMA
    any_space = pl.BlockSpec(memory_space=pl.ANY)
    vmem_space = pl.BlockSpec(memory_space=pltpu.VMEM)
    mixed = pl.pallas_call(
        functools.partial(kernel, n_patch, n_head),
        out_shape=jax.ShapeDtypeStruct((columns, rows), BF16),
        in_specs=[any_space] * 9,
        out_specs=vmem_space,
        scratch_shapes=[
            pltpu.VMEM((channels,), F32),
            pltpu.VMEM((channels,), F32),
            pltpu.VMEM((rows, channels), BF16),
            pltpu.VMEM((rows, inner), BF16),
            pltpu.VMEM((channels, inner), BF16),
            pltpu.VMEM((channels, inner), BF16),
            pltpu.VMEM((channels, inner), BF16),
            pltpu.VMEM((n_head, pairs, LANES, wide), BF16),
            pltpu.VMEM((pairs, wide, n_head * LANES), BF16),
            pltpu.VMEM((channels, LANES), BF16),
            pltpu.VMEM((pairs, 2 * n_z + 1, 2, rows, LANES), BF16),
            pltpu.VMEM((X, pairs, rows, LANES), BF16),
            pltpu.VMEM((pairs, X, rows + 16, LANES), BF16),
            pltpu.VMEM((pairs, X, rows + 16, LANES), BF16),
            pltpu.VMEM((pairs, n_head * rows, LANES), BF16),
            pltpu.VMEM((2 * n_z * rows, 2 * LANES), F32),
            pltpu.VMEM((2 * n_z * rows, 2 * LANES), F32),
            pltpu.VMEM((2, 8, LANES), F32),
            pltpu.VMEM((X * CORES, 8, LANES), F32),
            pltpu.VMEM((n_z, 8, LANES), F32),
            dma((9,)),
            dma((2,)),
            dma((X * CORES,)),
            dma((X * CORES,)),
            dma((n_z,)),
            dma((n_z,)),
            dma((2, 2 * n_z)),
            dma((2, 2 * n_z)),
            dma((X, 2)),
            dma((X, 2)),
            dma((2, X)),
            dma((2, X)),
            dma((n_head,)),
            dma((n_head,)),
            dma((n_head,)),
            dma((n_head,)),
            dma((n_head, 2)),
            dma((n_head, 2)),
        ],
        compiler_params=pltpu.CompilerParams(
            collective_id=0, has_side_effects=True, vmem_limit_bytes=60 * 1024 * 1024
        ),
    )(*operands)
    return jnp.transpose(mixed)


def solution(mesh):
    in_specs = (
        P(("cfg", "patch"), None),
        P(),
        P(),
        P(None, "head"),
        P(None, "head"),
        P(None, "head"),
        P("head", None),
        P(("cfg", "patch"), "head"),
        P(("cfg", "patch"), "head"),
    )
    return jax.shard_map(
        functools.partial(per_device, mesh.shape["patch"], mesh.shape["head"]),
        mesh=mesh,
        in_specs=in_specs,
        out_specs=P(("cfg", "patch"), "head"),
        check_vma=False,
    )
```

```python
import functools

import jax
import jax.numpy as jnp
from jax import lax
from jax.experimental import pallas as pl
from jax.experimental.pallas import tpu as pltpu
from jax.sharding import PartitionSpec as P

HEAD_DIM = 64
GROUPS = 32
EPSILON = 1e-06
X = 4
CORES = 2
LANES = 128
MESH = pl.DeviceIdType.MESH
NT = (((1,), (1,)), ((), ()))
F32 = jnp.float32
BF16 = jnp.bfloat16


def three_parts(value):
    high = value.astype(BF16).astype(F32)
    rest = value - high
    middle = rest.astype(BF16).astype(F32)
    low = (rest - middle).astype(BF16).astype(F32)
    return [high, middle, low]


def stack_rows(rows, height):
    width = rows[0].shape[1]
    index = lax.broadcasted_iota(jnp.int32, (height, width), 0)
    stacked = jnp.zeros((height, width), F32)
    for i, row in enumerate(rows):
        stacked = jnp.where(index == i, row, stacked)
    return stacked.astype(BF16)


def kernel(
    n_patch,
    n_head,
    tokens,
    gain,
    bias,
    w_query,
    w_key,
    w_value,
    w_out,
    stale_keys,
    stale_values,
    out,
    gain_v,
    bias_v,
    tok_v,
    stv_v,
    wq_v,
    wk_v,
    wv_v,
    wo_all,
    wo_t,
    groups_v,
    kv,
    qbuf,
    osend,
    obuf,
    att,
    scores_a,
    scores_b,
    st_send,
    st_a,
    st_b,
    ld_sem,
    wo_ld_sem,
    sta_send,
    sta_recv,
    stb_send,
    stb_recv,
    kz_send,
    kz_recv,
    kc_send,
    kc_recv,
    q_send,
    q_recv,
    o_send,
    o_recv,
    wo_send,
    wo_recv,
    wf_send,
    wf_recv,
    att_send,
    att_recv,
    near_sem,
    far_head_sem,
):
    n_z = n_patch // (X * CORES)
    plane = X * CORES
    rows, channels = tok_v.shape
    per_group = channels // GROUPS
    own_stale = 2 * n_z
    me = lax.axis_index("patch")
    head = lax.axis_index("head")
    z = me // plane
    x = (me // CORES) % X
    core = me % CORES
    columns = channels // n_head
    wide = wo_all.shape[3]

    def at(zz, xx, cc):
        return {"patch": (zz * X + xx) * CORES + cc}

    def z_peer(k):
        return at((z + k) % n_z, x, core)

    def x_peer(k):
        return at(z, (x + k) % X, core)

    def plane_peer(k):
        rank = (x * CORES + core + k) % plane
        return {"patch": z * plane + rank}

    def head_peer(k):
        return {"head": (head + k) % n_head}

    sibling = at(z, x, 1 - core)

    def remote(src, dst, send, recv, device):
        return pltpu.make_async_remote_copy(
            src_ref=src, dst_ref=dst, send_sem=send, recv_sem=recv, device_id=device, device_id_type=MESH
        )

    barrier = pltpu.get_barrier_semaphore()
    peers = [plane_peer(k) for k in range(1, plane)]
    peers += [z_peer(1), z_peer(n_z - 1), head_peer(1), head_peer(n_head - 1)]
    for peer in peers:
        pl.semaphore_signal(barrier, inc=1, device_id=peer, device_id_type=MESH)

    def load(source, target, sem):
        copy = pltpu.make_async_copy(source, target, sem)
        copy.start()
        return copy

    load_stale = [
        load(stale_keys.at[:, p * LANES : (p + 1) * LANES], kv.at[p, own_stale, 0], ld_sem.at[1 + p]) for p in range(2)
    ]
    load_stale.append(load(stale_values, stv_v, ld_sem.at[3]))
    load_tok = load(tokens, tok_v, ld_sem.at[0])
    load_norm = [load(gain, gain_v, ld_sem.at[4]), load(bias, bias_v, ld_sem.at[5])]
    load_w = [
        load(source, target, ld_sem.at[6 + i])
        for i, (source, target) in enumerate(((w_query, wq_v), (w_key, wk_v), (w_value, wv_v)))
    ]

    def first_column(h):
        return pl.multiple_of((h * columns) // LANES * LANES, LANES)

    load_wo = [
        load(
            w_out.at[p * LANES : (p + 1) * LANES, pl.ds(first_column(head), wide)], wo_all.at[0, p], wo_ld_sem.at[p]
        )
        for p in range(2)
    ]

    hops = n_z // 2

    def z_copy(p, which, src, dst, k):
        return remote(
            kv.at[p, src, which], kv.at[p, dst, which], kz_send.at[p, dst, which], kz_recv.at[p, dst, which], z_peer(k)
        )

    def core_copy(p, src, dst):
        return remote(kv.at[p, src], kv.at[p, dst], kc_send.at[p, dst], kc_recv.at[p, dst], sibling)

    def from_core(p, slot):
        core_copy(p, own_stale, slot).wait_recv()

    def kv_first(p, which):
        z_copy(p, which, own_stale, 2, 1).start()
        z_copy(p, which, own_stale, 3, n_z - 1).start()

    def kv_forward(p, hop):
        below, above = 4 * hop - 2, 4 * hop - 1
        if hop == hops:
            for which in range(2):
                z_copy(p, which, own_stale, below, 1).wait_recv()
            core_copy(p, below, below + 1).start()
            return
        for which in range(2):
            z_copy(p, which, own_stale, below, 1).wait_recv()
            if hop + 1 < hops or which == 0:
                z_copy(p, which, below, below + 4, 1).start()
            z_copy(p, which, own_stale, above, 1).wait_recv()
            if hop + 1 < hops:
                z_copy(p, which, above, above + 4, n_z - 1).start()
            elif which == 1:
                z_copy(p, which, above, below + 4, n_z - 1).start()
        core_copy(p, below, below + 2).start()
        core_copy(p, above, above + 2).start()

    pl.semaphore_wait(barrier, len(peers))

    def pass_on(rounds, up, down):
        if up:
            pl.semaphore_signal(near_sem.at[0, rounds], inc=1, device_id=z_peer(1), device_id_type=MESH)
        if down:
            pl.semaphore_signal(near_sem.at[1, rounds], inc=1, device_id=z_peer(n_z - 1), device_id_type=MESH)

    def learn(rounds, up, down):
        if up:
            pl.semaphore_wait(near_sem.at[0, rounds], 1)
        if down:
            pl.semaphore_wait(near_sem.at[1, rounds], 1)

    pass_on(0, True, True)
    pl.semaphore_signal(far_head_sem, inc=1, device_id=head_peer(1), device_id_type=MESH)
    load_stale[0].wait()
    kv_first(0, 0)
    load_stale[2].wait()
    for p in range(2):
        kv[p, own_stale, 1] = jnp.transpose(stv_v[:, p * LANES : (p + 1) * LANES])
    kv_first(0, 1)
    load_stale[1].wait()
    kv_first(1, 0)
    kv_first(1, 1)
    for p in range(2):
        core_copy(p, own_stale, 1).start()

    channel = lax.broadcasted_iota(jnp.int32, (channels, LANES), 0)
    first = lax.broadcasted_iota(jnp.int32, (channels, LANES), 1) * per_group
    groups_v[...] = ((channel >= first) & (channel < first + per_group)).astype(F32).astype(BF16)

    def to_groups(row):
        parts = jnp.dot(stack_rows(three_parts(row), 16), groups_v[...], preferred_element_type=F32)
        return jnp.sum(parts, axis=0, keepdims=True)

    def to_channels(*values):
        stacked = stack_rows([part for value in values for part in three_parts(value)], 16)
        spread = lax.dot_general(stacked, groups_v[...], NT, preferred_element_type=F32)
        return [
            spread[3 * i : 3 * i + 1] + spread[3 * i + 1 : 3 * i + 2] + spread[3 * i + 2 : 3 * i + 3]
            for i in range(len(values))
        ]

    load_tok.wait()
    own_count = rows * per_group
    own_mean = to_groups(jnp.sum(tok_v[...].astype(F32), axis=0, keepdims=True)) * (1.0 / own_count)
    (shift,) = to_channels(own_mean)
    centred = tok_v[...].astype(F32) - shift
    own_squares = to_groups(jnp.sum(centred * centred, axis=0, keepdims=True))

    index8 = lax.broadcasted_iota(jnp.int32, (8, LANES), 0)

    def packet(mean, squares):
        return jnp.where(index8 == 0, mean, jnp.where(index8 == 1, squares, 0.0))

    def join(stats, count):
        shares = stats.shape[0]
        total = jnp.sum(stats, axis=0)
        mean = total * (1.0 / shares)
        apart = stats - mean[None]
        spread = jnp.sum(apart * apart, axis=0)
        return mean[0:1], total[1:2] + count * spread[0:1]

    own_packet = packet(own_mean, own_squares)
    st_send[0] = own_packet
    st_a[0] = own_packet
    learn(0, True, True)
    pass_on(1, True, True)
    stat_a = [
        remote(st_send.at[0], st_a.at[k], sta_send.at[k], sta_recv.at[k], plane_peer(k)) for k in range(1, plane)
    ]
    for copy in stat_a:
        copy.start()

    def wo_copy(k):
        return remote(
            w_out.at[pl.ds(core * LANES, LANES), pl.ds(first_column((head + k) % n_head), wide)],
            wo_all.at[n_head - k, core],
            wo_send.at[n_head - k],
            wo_recv.at[n_head - k],
            head_peer(k),
        )

    def wo_forward(s):
        return remote(wo_all.at[s, core], wo_all.at[s, core], wf_send.at[s], wf_recv.at[s], sibling)

    def wo_from_sibling(s):
        return remote(wo_all.at[s, core], wo_all.at[s, 1 - core], wf_send.at[s], wf_recv.at[s], sibling)

    pl.semaphore_wait(far_head_sem, 1)
    for k in range(1, n_head):
        wo_copy(k).start()

    kv_forward(0, 1)
    learn(1, True, True)
    pass_on(2, True, False)
    kv_forward(1, 1)
    for copy in stat_a:
        copy.wait_recv()
    mean, squares = join(st_a[...], own_count)
    plane_packet = packet(mean, squares)
    st_send[1] = plane_packet
    st_b[0] = plane_packet
    far_first = sorted(range(1, n_z), key=lambda k: -min(k, n_z - k))
    stat_b = [remote(st_send.at[1], st_b.at[k], stb_send.at[k], stb_recv.at[k], z_peer(k)) for k in far_first]
    learn(2, True, False)
    for copy in stat_b:
        copy.start()

    for copy in load_norm + load_w:
        copy.wait()
    kv_forward(0, 2)
    kv_forward(1, 2)
    kv_forward(0, 3)

    for copy in stat_b:
        copy.wait_recv()
    mean, squares = join(st_b[...], own_count * plane)
    inverse = lax.rsqrt(squares * (1.0 / (own_count * n_patch)) + EPSILON)
    mean_of, inverse_of = to_channels(mean, inverse)
    normed = (tok_v[...].astype(F32) - mean_of) * inverse_of
    normed = (normed * gain_v[...].reshape(1, channels) + bias_v[...].reshape(1, channels)).astype(BF16)

    query = jnp.dot(normed, wq_v[...], preferred_element_type=F32).astype(BF16) * jnp.asarray(0.125, BF16)
    for p in range(2):
        qbuf[0, p] = query[:, p * LANES : (p + 1) * LANES]

    def q_copy(p, k):
        return remote(qbuf.at[0, p], qbuf.at[X - k, p], q_send.at[X - k, p], q_recv.at[X - k, p], x_peer(k))

    for p in range(2):
        for k in range(X - 1, 0, -1):
            q_copy(p, k).start()

    kv_forward(1, 3)

    fresh = jnp.dot(normed, wk_v[...], preferred_element_type=F32).astype(BF16)
    for p in range(2):
        kv[p, 0, 0] = fresh[:, p * LANES : (p + 1) * LANES]
    fresh = jnp.dot(normed, wv_v[...], preferred_element_type=F32)
    for p in range(2):
        kv[p, 0, 1] = jnp.transpose(fresh[:, p * LANES : (p + 1) * LANES]).astype(BF16)

    lane = lax.broadcasted_iota(jnp.int32, (rows, LANES), 1)
    blocks = 2
    span = blocks * rows
    chunks = 2 * n_z // blocks
    both = 2 * LANES

    def masked_queries(p, j):
        q = qbuf[j, p]
        return jnp.concatenate(
            [jnp.where((lane < HEAD_DIM) == (h == 0), q, jnp.zeros_like(q)) for h in range(2)], axis=0
        )

    def slots_of(j, c):
        return [slot if slot else (own_stale if j else 0) for slot in range(blocks * c, blocks * (c + 1))]

    def scores_of(p, j, queries, c):
        keys = jnp.concatenate([kv[p, slot, 0] for slot in slots_of(j, c)], axis=0)
        return lax.dot_general(keys, queries, NT, preferred_element_type=F32)

    def by_sublane(reduce, value):
        return reduce(value.reshape(span // 8, 8, both), axis=0)

    def score_chunk(p, j, queries, c, scores_ref):
        scores = scores_of(p, j, queries, c)
        scores_ref[c * span : (c + 1) * span] = scores
        return by_sublane(jnp.max, scores)

    def weigh(p, j, weights, c):
        values = jnp.concatenate([kv[p, slot, 1] for slot in slots_of(j, c)], axis=1)
        summed = jnp.dot(values, weights.astype(BF16), preferred_element_type=F32)
        return by_sublane(jnp.sum, weights), summed

    def sum_chunk(p, j, top, c, scores_ref):
        return weigh(p, j, jnp.exp(scores_ref[c * span : (c + 1) * span] - top), c)

    def o_copy(p, j):
        return remote(osend.at[p, j], obuf.at[p, X - j], o_send.at[p, j], o_recv.at[p, X - j], x_peer(j))

    def q_arrived(p, j):
        remote(qbuf.at[0, p], qbuf.at[j, p], q_send.at[j, p], q_recv.at[j, p], sibling).wait_recv()

    def finish(p, j, top, total, summed):
        summed = summed * (1.0 / total)
        logs = top + jnp.log(total)
        osend[p, j, :rows] = jnp.concatenate(
            [summed[:HEAD_DIM, :LANES], summed[HEAD_DIM:, LANES:]], axis=0
        ).astype(BF16)
        three = three_parts(logs)
        osend[p, j, rows:] = stack_rows(
            [part[:, h * LANES : (h + 1) * LANES] for part in three for h in range(2)], 16
        )
        if j:
            o_copy(p, j).start()

    def att_copy(p, k):
        own = att.at[p, 0:rows]
        there = att.at[p, (n_head - k) * rows : (n_head - k + 1) * rows]
        return remote(own, there, att_send.at[n_head - k, p], att_recv.at[n_head - k, p], head_peer(k))

    def combine(p):
        for s in range(1, X):
            o_copy(p, X - s).wait_recv()
        partials = [osend[p, 0]] + [obuf[p, s] for s in range(1, X)]
        logs = []
        for partial in partials:
            parts = partial[rows:].astype(F32)
            logs.append([parts[h : h + 1] + parts[2 + h : 3 + h] + parts[4 + h : 5 + h] for h in range(2)])
        joined = []
        for h in range(2):
            top = functools.reduce(jnp.maximum, [value[h] for value in logs])
            share = [jnp.exp(value[h] - top) for value in logs]
            inverse_total = 1.0 / functools.reduce(jnp.add, share)
            terms = [
                partial[h * HEAD_DIM : (h + 1) * HEAD_DIM].astype(F32) * (value * inverse_total)
                for partial, value in zip(partials, share)
            ]
            joined.append(functools.reduce(jnp.add, terms))
        att[p, 0:rows] = jnp.concatenate(joined, axis=0).astype(BF16)
        for k in sorted(range(1, n_head), key=lambda k: -min(k, n_head - k)):
            att_copy(p, k).start()

    core_slots = [slot for slot in range(1, 2 * n_z) if slot in (1, 2 * n_z - 1) or slot % 4 < 2]
    last = chunks - 1

    order = [(0, 0), (1, 0), (0, 1), (0, 2), (0, 3), (1, 2), (1, 1), (1, 3)]
    early = 6
    buffers = (scores_a, scores_b)

    def arrive(i):
        p, j = order[i]
        if j:
            q_arrived(p, j)
        elif i:
            for slot in core_slots[:-1]:
                from_core(p, slot)

    state = {}
    tops, queries_of = {}, {}

    def first_pass(i, c, top, buffer):
        p, j = order[i]
        more = score_chunk(p, j, queries_of[i], c, buffer)
        return more if top is None else jnp.maximum(top, more)

    def run(units):
        for n, i in enumerate(units):
            p, j = order[i]
            after = units[n + 1] if n + 1 < len(units) else None
            count = last if i < early else chunks
            after_count = 0 if after is None else last if after < early else chunks
            if after is not None:
                arrive(after)
                queries_of[after] = masked_queries(*order[after])
            next_top, total, summed = None, None, None
            for c in range(max(count, after_count)):
                if c < after_count:
                    next_top = first_pass(after, c, next_top, buffers[(n + 1) % 2])
                if c < count:
                    more, term = sum_chunk(p, j, tops[i], c, buffers[n % 2])
                    total = more if total is None else total + more
                    summed = term if summed is None else summed + term
            total = jnp.sum(total, axis=0, keepdims=True)
            if after is not None:
                tops[after] = jnp.max(next_top, axis=0, keepdims=True)
            if i < early:
                state[i] = (tops[i], total, summed)
            else:
                finish(p, j, tops[i], total, summed)
            if n == 1 and i < early:
                kv_forward(0, hops)
                kv_forward(1, hops)

    def complete(units):
        scores = [scores_of(*order[i], queries_of[i], last) for i in units]
        for i, score in zip(units, scores):
            p, j = order[i]
            top, total, summed = state[i]
            new_top = jnp.maximum(top, jnp.max(score, axis=0, keepdims=True))
            factor = jnp.exp(top - new_top)
            more, term = weigh(p, j, jnp.exp(score - new_top), last)
            total = total * factor + jnp.sum(more, axis=0, keepdims=True)
            finish(p, j, new_top, total, summed * factor + term)

    queries_of[0] = masked_queries(*order[0])
    top = None
    for c in range(last):
        for slot in range(blocks * c, blocks * (c + 1)):
            if slot in core_slots:
                from_core(0, slot)
        top = first_pass(0, c, top, scores_a)
    tops[0] = jnp.max(top, axis=0, keepdims=True)
    run(list(range(early)))
    for p in range(2):
        from_core(p, 2 * n_z - 1)
    complete([i for i in range(2, early)])
    arrive(early)
    queries_of[early] = masked_queries(*order[early])
    top = None
    for c in range(chunks):
        top = first_pass(early, c, top, scores_a)
    tops[early] = jnp.max(top, axis=0, keepdims=True)
    run(list(range(early, len(order))))
    for s in range(1, n_head):
        wo_copy(n_head - s).wait_recv()
        wo_forward(s).start()
    complete([0, 1])
    combine(0)

    for copy in load_wo:
        copy.wait()
    for s in range(1, n_head):
        wo_from_sibling(s).wait_recv()
    for p in range(2):
        for s in range(n_head):
            wo_t[p, :, s * LANES : (s + 1) * LANES] = jnp.transpose(wo_all[s, p])
    for copy in stat_a + stat_b:
        copy.wait_send()
    for p in range(2):
        for slot in range(2, 2 * n_z - 1):
            if slot not in core_slots:
                for which in range(2):
                    z_copy(p, which, own_stale, slot, 1).wait_send()
        for slot in core_slots:
            core_copy(p, own_stale, slot).wait_send()
        for k in range(1, X):
            q_copy(p, k).wait_send()
            o_copy(p, k).wait_send()
    for k in range(1, n_head):
        wo_copy(k).wait_send()
        wo_forward(k).wait_send()
    combine(1)

    mixed = None
    for p in range(2):
        for s in range(1, n_head):
            att_copy(p, n_head - s).wait_recv()
        term = jnp.dot(wo_t[p], att[p], preferred_element_type=F32)
        mixed = term if mixed is None else mixed + term
    shift = (head * columns) % LANES
    half = LANES // 2
    out[...] = jnp.where(shift == 0, mixed[:columns], mixed[half : half + columns]).astype(BF16)

    for p in range(2):
        for k in range(1, n_head):
            att_copy(p, k).wait_send()


def per_device(n_patch, n_head, *operands):
    tokens, _, _, w_query = operands[:4]
    rows, channels = tokens.shape
    inner = w_query.shape[1]
    n_z = n_patch // (X * CORES)
    columns = channels // n_head
    wide = -(-(columns + LANES // 2) // LANES) * LANES
    pairs = inner // LANES
    dma = pltpu.SemaphoreType.DMA
    any_space = pl.BlockSpec(memory_space=pl.ANY)
    vmem_space = pl.BlockSpec(memory_space=pltpu.VMEM)
    mixed = pl.pallas_call(
        functools.partial(kernel, n_patch, n_head),
        out_shape=jax.ShapeDtypeStruct((columns, rows), BF16),
        in_specs=[any_space] * 9,
        out_specs=vmem_space,
        scratch_shapes=[
            pltpu.VMEM((channels,), F32),
            pltpu.VMEM((channels,), F32),
            pltpu.VMEM((rows, channels), BF16),
            pltpu.VMEM((rows, inner), BF16),
            pltpu.VMEM((channels, inner), BF16),
            pltpu.VMEM((channels, inner), BF16),
            pltpu.VMEM((channels, inner), BF16),
            pltpu.VMEM((n_head, pairs, LANES, wide), BF16),
            pltpu.VMEM((pairs, wide, n_head * LANES), BF16),
            pltpu.VMEM((channels, LANES), BF16),
            pltpu.VMEM((pairs, 2 * n_z + 1, 2, rows, LANES), BF16),
            pltpu.VMEM((X, pairs, rows, LANES), BF16),
            pltpu.VMEM((pairs, X, rows + 16, LANES), BF16),
            pltpu.VMEM((pairs, X, rows + 16, LANES), BF16),
            pltpu.VMEM((pairs, n_head * rows, LANES), BF16),
            pltpu.VMEM((2 * n_z * rows, 2 * LANES), F32),
            pltpu.VMEM((2 * n_z * rows, 2 * LANES), F32),
            pltpu.VMEM((2, 8, LANES), F32),
            pltpu.VMEM((X * CORES, 8, LANES), F32),
            pltpu.VMEM((n_z, 8, LANES), F32),
            dma((9,)),
            dma((2,)),
            dma((X * CORES,)),
            dma((X * CORES,)),
            dma((n_z,)),
            dma((n_z,)),
            dma((2, 2 * n_z, 2)),
            dma((2, 2 * n_z, 2)),
            dma((2, 2 * n_z)),
            dma((2, 2 * n_z)),
            dma((X, 2)),
            dma((X, 2)),
            dma((2, X)),
            dma((2, X)),
            dma((n_head,)),
            dma((n_head,)),
            dma((n_head,)),
            dma((n_head,)),
            dma((n_head, 2)),
            dma((n_head, 2)),
            pltpu.SemaphoreType.REGULAR((2, 3)),
            pltpu.SemaphoreType.REGULAR,
        ],
        compiler_params=pltpu.CompilerParams(
            collective_id=0, has_side_effects=True, vmem_limit_bytes=40 * 1024 * 1024
        ),
    )(*[pltpu.with_memory_space_constraint(operand, pltpu.HBM) for operand in operands])
    return jnp.transpose(mixed)


def solution(mesh):
    in_specs = (
        P(("cfg", "patch"), None),
        P(),
        P(),
        P(None, "head"),
        P(None, "head"),
        P(None, "head"),
        P("head", None),
        P(("cfg", "patch"), "head"),
        P(("cfg", "patch"), "head"),
    )
    return jax.shard_map(
        functools.partial(per_device, mesh.shape["patch"], mesh.shape["head"]),
        mesh=mesh,
        in_specs=in_specs,
        out_specs=P(("cfg", "patch"), "head"),
        check_vma=False,
    )
```

```python
import functools

import jax
import jax.numpy as jnp
from jax import lax
from jax.experimental import pallas as pl
from jax.experimental.pallas import tpu as pltpu
from jax.sharding import PartitionSpec as P

HEAD_DIM = 64
GROUPS = 32
EPSILON = 1e-06
X = 4
CORES = 2
LANES = 128
MESH = pl.DeviceIdType.MESH
NT = (((1,), (1,)), ((), ()))
F32 = jnp.float32
BF16 = jnp.bfloat16


def three_parts(value):
    high = value.astype(BF16).astype(F32)
    rest = value - high
    middle = rest.astype(BF16).astype(F32)
    low = (rest - middle).astype(BF16).astype(F32)
    return [high, middle, low]


def stack_rows(rows, height):
    width = rows[0].shape[1]
    index = lax.broadcasted_iota(jnp.int32, (height, width), 0)
    stacked = jnp.zeros((height, width), F32)
    for i, row in enumerate(rows):
        stacked = jnp.where(index == i, row, stacked)
    return stacked.astype(BF16)


def kernel(
    n_patch,
    n_head,
    tokens,
    gain,
    bias,
    w_query,
    w_key,
    w_value,
    w_out,
    stale_keys,
    stale_values,
    out,
    gain_v,
    bias_v,
    tok_v,
    stv_v,
    wq_v,
    wk_v,
    wv_v,
    wo_all,
    wo_t,
    groups_v,
    keys_v,
    values_v,
    qbuf,
    osend,
    obuf,
    att,
    scores_a,
    scores_b,
    st_send,
    st_a,
    st_b,
    ld_sem,
    wo_ld_sem,
    sib_send,
    sib_recv,
    sta_send,
    sta_recv,
    stb_send,
    stb_recv,
    kz_send,
    kz_recv,
    q_send,
    q_recv,
    o_send,
    o_recv,
    wo_send,
    wo_recv,
    wf_send,
    wf_recv,
    att_send,
    att_recv,
    near_sem,
    far_head_sem,
):
    n_z = n_patch // (X * CORES)
    plane = X * CORES
    rows, channels = tokens.shape
    chip_rows = CORES * rows
    per_group = channels // GROUPS
    fresh_slot = n_z
    me = lax.axis_index("patch")
    head = lax.axis_index("head")
    z = me // plane
    x = (me // CORES) % X
    core = me % CORES
    columns = channels // n_head
    wide = wo_all.shape[3]

    def at(zz, xx, cc):
        return {"patch": (zz * X + xx) * CORES + cc}

    def z_peer(k):
        return at((z + k) % n_z, x, core)

    def x_peer(k):
        return at(z, (x + k) % X, core)

    def plane_peer(k):
        rank = (x * CORES + core + k) % plane
        return {"patch": z * plane + rank}

    def head_peer(k):
        return {"head": (head + k) % n_head}

    sibling = at(z, x, 1 - core)

    def remote(src, dst, send, recv, device):
        return pltpu.make_async_remote_copy(
            src_ref=src, dst_ref=dst, send_sem=send, recv_sem=recv, device_id=device, device_id_type=MESH
        )

    barrier = pltpu.get_barrier_semaphore()
    peers = [plane_peer(k) for k in range(1, plane)]
    peers += [z_peer(1), z_peer(n_z - 1), head_peer(1), head_peer(n_head - 1)]
    for peer in peers:
        pl.semaphore_signal(barrier, inc=1, device_id=peer, device_id_type=MESH)

    def load(source, target, sem):
        copy = pltpu.make_async_copy(source, target, sem)
        copy.start()
        return copy

    own_pair = pl.ds(pl.multiple_of(core * LANES, LANES), LANES)
    other_pair = pl.ds(pl.multiple_of((1 - core) * LANES, LANES), LANES)
    load_tok = load(tokens, tok_v.at[0:rows], ld_sem.at[0])
    load_stale = [
        load(stale_keys.at[:, own_pair], keys_v.at[0, 0:rows], ld_sem.at[1]),
        load(stale_values.at[:, own_pair], stv_v.at[0:rows], ld_sem.at[2]),
    ]
    load_norm = [load(gain, gain_v, ld_sem.at[4]), load(bias, bias_v, ld_sem.at[5])]
    load_w = [
        load(source.at[:, own_pair], target, ld_sem.at[6 + i])
        for i, (source, target) in enumerate(((w_query, wq_v), (w_key, wk_v), (w_value, wv_v)))
    ]

    def first_column(h):
        return pl.multiple_of((h * columns) // LANES * LANES, LANES)

    load_wo = [
        load(
            w_out.at[pl.ds((core + r - 2 * core * r) * LANES, LANES), pl.ds(first_column(head), wide)],
            wo_all.at[0, r],
            wo_ld_sem.at[r],
        )
        for r in range(2)
    ]

    hops = n_z // 2
    held = (keys_v, values_v)

    def z_copy(which, src, dst, k):
        ref = held[which]
        return remote(ref.at[src], ref.at[dst], kz_send.at[dst, which], kz_recv.at[dst, which], z_peer(k))

    def kv_first(which):
        z_copy(which, 0, 1, 1).start()
        z_copy(which, 0, 2, n_z - 1).start()

    def kv_arrived(which, slot):
        z_copy(which, 0, slot, 1).wait_recv()

    def kv_forward(hop):
        below, above = 2 * hop - 1, 2 * hop
        for which in range(2):
            kv_arrived(which, below)
            if hop + 1 < hops or which == 0:
                z_copy(which, below, below + 2, 1).start()
            kv_arrived(which, above)
            if hop + 1 < hops:
                z_copy(which, above, above + 2, n_z - 1).start()
            elif which == 1:
                z_copy(which, above, below + 2, n_z - 1).start()

    channel = lax.broadcasted_iota(jnp.int32, (channels, LANES), 0)
    first = lax.broadcasted_iota(jnp.int32, (channels, LANES), 1) * per_group
    groups_v[...] = ((channel >= first) & (channel < first + per_group)).astype(F32).astype(BF16)

    def to_groups(row):
        parts = jnp.dot(stack_rows(three_parts(row), 16), groups_v[...], preferred_element_type=F32)
        return jnp.sum(parts, axis=0, keepdims=True)

    def to_channels(*values):
        stacked = stack_rows([part for value in values for part in three_parts(value)], 16)
        spread = lax.dot_general(stacked, groups_v[...], NT, preferred_element_type=F32)
        return [
            spread[3 * i : 3 * i + 1] + spread[3 * i + 1 : 3 * i + 2] + spread[3 * i + 2 : 3 * i + 3]
            for i in range(len(values))
        ]

    load_tok.wait()
    own_count = rows * per_group
    own_mean = to_groups(jnp.sum(tok_v[0:rows].astype(F32), axis=0, keepdims=True)) * (1.0 / own_count)
    (shift,) = to_channels(own_mean)
    centred = tok_v[0:rows].astype(F32) - shift
    own_squares = to_groups(jnp.sum(centred * centred, axis=0, keepdims=True))

    index8 = lax.broadcasted_iota(jnp.int32, (8, LANES), 0)

    def packet(mean, squares):
        return jnp.where(index8 == 0, mean, jnp.where(index8 == 1, squares, 0.0))

    def join(stats, count):
        shares = stats.shape[0]
        total = jnp.sum(stats, axis=0)
        mean = total * (1.0 / shares)
        apart = stats - mean[None]
        spread = jnp.sum(apart * apart, axis=0)
        return mean[0:1], total[1:2] + count * spread[0:1]

    own_packet = packet(own_mean, own_squares)
    st_send[0] = own_packet
    st_a[0] = own_packet
    pl.semaphore_wait(barrier, len(peers))

    def pass_on(rounds, up, down):
        if up:
            pl.semaphore_signal(near_sem.at[0, rounds], inc=1, device_id=z_peer(1), device_id_type=MESH)
        if down:
            pl.semaphore_signal(near_sem.at[1, rounds], inc=1, device_id=z_peer(n_z - 1), device_id_type=MESH)

    def learn(rounds, up, down):
        if up:
            pl.semaphore_wait(near_sem.at[0, rounds], 1)
        if down:
            pl.semaphore_wait(near_sem.at[1, rounds], 1)

    pass_on(0, True, True)
    pl.semaphore_signal(far_head_sem, inc=1, device_id=head_peer(1), device_id_type=MESH)
    to_sibling = [
        remote(stale_keys.at[:, other_pair], keys_v.at[0, rows:chip_rows], sib_send.at[0], sib_recv.at[0], sibling),
        remote(stale_values.at[:, other_pair], stv_v.at[rows:chip_rows], sib_send.at[1], sib_recv.at[1], sibling),
        remote(tokens, tok_v.at[rows:chip_rows], sib_send.at[2], sib_recv.at[2], sibling),
    ]
    for copy in to_sibling:
        copy.start()
    learn(0, True, True)
    pass_on(1, True, True)
    stat_a = [
        remote(st_send.at[0], st_a.at[k], sta_send.at[k], sta_recv.at[k], plane_peer(k)) for k in range(1, plane)
    ]
    for copy in stat_a:
        copy.start()
    load_stale[0].wait()
    to_sibling[0].wait_recv()
    kv_first(0)
    load_stale[1].wait()
    to_sibling[1].wait_recv()
    values_v[0] = jnp.transpose(stv_v[...])
    kv_first(1)


    def wo_copy(k):
        return remote(
            w_out.at[pl.ds(core * LANES, LANES), pl.ds(first_column((head + k) % n_head), wide)],
            wo_all.at[n_head - k, 0],
            wo_send.at[n_head - k],
            wo_recv.at[n_head - k],
            head_peer(k),
        )

    def wo_forward(s):
        return remote(wo_all.at[s, 0], wo_all.at[s, 1], wf_send.at[s], wf_recv.at[s], sibling)

    pl.semaphore_wait(far_head_sem, 1)
    for k in range(1, n_head):
        wo_copy(k).start()

    learn(1, True, True)
    pass_on(2, True, False)
    for copy in stat_a:
        copy.wait_recv()
    mean, squares = join(st_a[...], own_count)
    plane_packet = packet(mean, squares)
    st_send[1] = plane_packet
    st_b[0] = plane_packet
    far_first = sorted(range(1, n_z), key=lambda k: -min(k, n_z - k))
    stat_b = [remote(st_send.at[1], st_b.at[k], stb_send.at[k], stb_recv.at[k], z_peer(k)) for k in far_first]
    learn(2, True, False)
    for copy in stat_b:
        copy.start()

    for copy in load_norm + load_w:
        copy.wait()
    kv_forward(1)
    kv_forward(2)
    to_sibling[2].wait_recv()

    for copy in stat_b:
        copy.wait_recv()
    mean, squares = join(st_b[...], own_count * plane)
    inverse = lax.rsqrt(squares * (1.0 / (own_count * n_patch)) + EPSILON)
    mean_of, inverse_of = to_channels(mean, inverse)
    normed = (tok_v[...].astype(F32) - mean_of) * inverse_of
    normed = (normed * gain_v[...].reshape(1, channels) + bias_v[...].reshape(1, channels)).astype(BF16)

    query = jnp.dot(normed, wq_v[...], preferred_element_type=F32).astype(BF16) * jnp.asarray(0.125, BF16)
    qbuf[0] = query

    def q_copy(k, t):
        part = slice(t * rows, (t + 1) * rows)
        there = X - k
        return remote(qbuf.at[0, part], qbuf.at[there, part], q_send.at[there, t], q_recv.at[there, t], x_peer(k))

    for t in range(CORES):
        for k in range(X - 1, 0, -1):
            q_copy(k, t).start()

    keys_v[fresh_slot] = jnp.dot(normed, wk_v[...], preferred_element_type=F32).astype(BF16)
    fresh = jnp.dot(normed, wv_v[...], preferred_element_type=F32)
    values_v[fresh_slot] = jnp.transpose(fresh).astype(BF16)
    kv_forward(3)
    lane = lax.broadcasted_iota(jnp.int32, (rows, LANES), 1)
    span = chip_rows
    chunks = n_z
    both = 2 * LANES

    def masked_queries(j, t):
        q = qbuf[j, t * rows : (t + 1) * rows]
        return jnp.concatenate(
            [jnp.where((lane < HEAD_DIM) == (h == 0), q, jnp.zeros_like(q)) for h in range(2)], axis=0
        )

    def slot_of(j, t, c, half):
        return fresh_slot if (j, c, half) == (0, 0, t) else c

    def keys_of(j, t, c):
        return jnp.concatenate(
            [keys_v[slot_of(j, t, c, half), half * rows : (half + 1) * rows] for half in range(CORES)], axis=0
        )

    def values_of(j, t, c):
        return jnp.concatenate(
            [values_v[slot_of(j, t, c, half), :, half * rows : (half + 1) * rows] for half in range(CORES)], axis=1
        )

    def scores_of(j, t, queries, c):
        return lax.dot_general(keys_of(j, t, c), queries, NT, preferred_element_type=F32)

    def by_sublane(reduce, value):
        return reduce(value.reshape(span // 8, 8, both), axis=0)

    def score_chunk(j, t, queries, c, scores_ref):
        scores = scores_of(j, t, queries, c)
        scores_ref[c * span : (c + 1) * span] = scores
        return by_sublane(jnp.max, scores)

    def weigh(j, t, weights, c):
        summed = jnp.dot(values_of(j, t, c), weights.astype(BF16), preferred_element_type=F32)
        return by_sublane(jnp.sum, weights), summed

    def sum_chunk(j, t, top, c, scores_ref):
        return weigh(j, t, jnp.exp(scores_ref[c * span : (c + 1) * span] - top), c)

    def o_copy(j, t):
        owner = at(z, (x + j) % X, core + t - 2 * core * t)
        there = (X - j) % X
        return remote(osend.at[j, t], obuf.at[t, there], o_send.at[j, t], o_recv.at[t, there], owner)

    def q_arrived(j, t):
        q_copy(X - j, t).wait_recv()

    def finish(j, t, top, total, summed):
        summed = summed * (1.0 / total)
        logs = top + jnp.log(total)
        osend[j, t, :rows] = jnp.concatenate(
            [summed[:HEAD_DIM, :LANES], summed[HEAD_DIM:, LANES:]], axis=0
        ).astype(BF16)
        three = three_parts(logs)
        osend[j, t, rows:] = stack_rows(
            [part[:, h * LANES : (h + 1) * LANES] for part in three for h in range(2)], 16
        )
        if j or t:
            o_copy(j, t).start()

    def att_copy(p, k):
        own = att.at[p, 0:rows]
        there = att.at[p, (n_head - k) * rows : (n_head - k + 1) * rows]
        return remote(own, there, att_send.at[n_head - k, p], att_recv.at[n_head - k, p], head_peer(k))

    def combine(p):
        for s in range(X):
            if s or p:
                o_copy((X - s) % X, p).wait_recv()
        partials = [obuf[p, s] if s or p else osend[0, 0] for s in range(X)]
        logs = []
        for partial in partials:
            parts = partial[rows:].astype(F32)
            logs.append([parts[h : h + 1] + parts[2 + h : 3 + h] + parts[4 + h : 5 + h] for h in range(2)])
        joined = []
        for h in range(2):
            top = functools.reduce(jnp.maximum, [value[h] for value in logs])
            share = [jnp.exp(value[h] - top) for value in logs]
            inverse_total = 1.0 / functools.reduce(jnp.add, share)
            terms = [
                partial[h * HEAD_DIM : (h + 1) * HEAD_DIM].astype(F32) * (value * inverse_total)
                for partial, value in zip(partials, share)
            ]
            joined.append(functools.reduce(jnp.add, terms))
        att[p, 0:rows] = jnp.concatenate(joined, axis=0).astype(BF16)
        for k in sorted(range(1, n_head), key=lambda k: -min(k, n_head - k)):
            att_copy(p, k).start()

    order = [(0, 0), (0, 1), (1, 0), (3, 0), (2, 0), (2, 1), (1, 1), (3, 1)]
    early = 5
    last = chunks - 1
    buffers = (scores_a, scores_b)
    state, tops, queries_of = {}, {}, {}

    def arrive(i):
        j, t = order[i]
        if j:
            q_arrived(j, t)
        queries_of[i] = masked_queries(j, t)

    def first_pass(i, c, top, buffer):
        more = score_chunk(*order[i], queries_of[i], c, buffer)
        return more if top is None else jnp.maximum(top, more)

    def count_of(i):
        return last if i < early else chunks

    def run(units):
        arrive(units[0])
        top = None
        for c in range(count_of(units[0])):
            top = first_pass(units[0], c, top, scores_a)
        tops[units[0]] = jnp.max(top, axis=0, keepdims=True)
        for n, i in enumerate(units):
            j, t = order[i]
            after = units[n + 1] if n + 1 < len(units) else None
            after_count = 0 if after is None else count_of(after)
            if after is not None:
                arrive(after)
            next_top, total, summed = None, None, None
            for c in range(max(count_of(i), after_count)):
                if c < after_count:
                    next_top = first_pass(after, c, next_top, buffers[(n + 1) % 2])
                if c < count_of(i):
                    more, term = sum_chunk(j, t, tops[i], c, buffers[n % 2])
                    total = more if total is None else total + more
                    summed = term if summed is None else summed + term
            total = jnp.sum(total, axis=0, keepdims=True)
            if after is not None:
                tops[after] = jnp.max(next_top, axis=0, keepdims=True)
            if i < early:
                state[i] = (tops[i], total, summed)
            else:
                finish(j, t, tops[i], total, summed)

    def complete(units):
        scores = [scores_of(*order[i], queries_of[i], last) for i in units]
        for i, score in zip(units, scores):
            j, t = order[i]
            top, total, summed = state[i]
            new_top = jnp.maximum(top, jnp.max(score, axis=0, keepdims=True))
            factor = jnp.exp(top - new_top)
            more, term = weigh(j, t, jnp.exp(score - new_top), last)
            total = total * factor + jnp.sum(more, axis=0, keepdims=True)
            finish(j, t, new_top, total, summed * factor + term)

    run(list(range(early)))
    for s in range(1, n_head):
        wo_copy(n_head - s).wait_recv()
        wo_forward(s).start()
    for which in range(2):
        kv_arrived(which, last)
    complete([i for i in range(2, early) if not order[i][1]])
    if early > X + 1:
        complete(list(range(X + 1, early)))
    if early < len(order):
        run(list(range(early, len(order))))
    complete([1, 0])
    combine(0)

    combine(1)

    for copy in load_wo:
        copy.wait()
    for s in range(1, n_head):
        wo_forward(s).wait_recv()
    for p in range(2):
        for s in range(n_head):
            wo_t[p, :, s * LANES : (s + 1) * LANES] = jnp.transpose(wo_all[s, p])
    for copy in stat_a + stat_b:
        copy.wait_send()
    for copy in to_sibling:
        copy.wait_send()
    for slot in range(1, n_z):
        for which in range(2):
            z_copy(which, 0, slot, 1).wait_send()
    for k in range(1, X):
        for t in range(CORES):
            q_copy(k, t).wait_send()
    for j, t in order[1:]:
        o_copy(j, t).wait_send()
    for k in range(1, n_head):
        wo_copy(k).wait_send()
        wo_forward(k).wait_send()

    mixed = None
    for p in range(2):
        for s in range(1, n_head):
            att_copy(p, n_head - s).wait_recv()
        term = jnp.dot(wo_t[p], att[p], preferred_element_type=F32)
        mixed = term if mixed is None else mixed + term
    shift = (head * columns) % LANES
    half = LANES // 2
    out[...] = jnp.where(shift == 0, mixed[:columns], mixed[half : half + columns]).astype(BF16)

    for p in range(2):
        for k in range(1, n_head):
            att_copy(p, k).wait_send()


def per_device(n_patch, n_head, *operands):
    tokens, _, _, w_query = operands[:4]
    rows, channels = tokens.shape
    inner = w_query.shape[1]
    n_z = n_patch // (X * CORES)
    columns = channels // n_head
    wide = -(-(columns + LANES // 2) // LANES) * LANES
    pairs = inner // LANES
    dma = pltpu.SemaphoreType.DMA
    any_space = pl.BlockSpec(memory_space=pl.ANY)
    vmem_space = pl.BlockSpec(memory_space=pltpu.VMEM)
    mixed = pl.pallas_call(
        functools.partial(kernel, n_patch, n_head),
        out_shape=jax.ShapeDtypeStruct((columns, rows), BF16),
        in_specs=[any_space] * 9,
        out_specs=vmem_space,
        scratch_shapes=[
            pltpu.VMEM((channels,), F32),
            pltpu.VMEM((channels,), F32),
            pltpu.VMEM((CORES * rows, channels), BF16),
            pltpu.VMEM((CORES * rows, LANES), BF16),
            pltpu.VMEM((channels, LANES), BF16),
            pltpu.VMEM((channels, LANES), BF16),
            pltpu.VMEM((channels, LANES), BF16),
            pltpu.VMEM((n_head, pairs, LANES, wide), BF16),
            pltpu.VMEM((pairs, wide, n_head * LANES), BF16),
            pltpu.VMEM((channels, LANES), BF16),
            pltpu.VMEM((n_z + 1, CORES * rows, LANES), BF16),
            pltpu.VMEM((n_z + 1, LANES, CORES * rows), BF16),
            pltpu.VMEM((X, CORES * rows, LANES), BF16),
            pltpu.VMEM((X, CORES, rows + 16, LANES), BF16),
            pltpu.VMEM((pairs, X, rows + 16, LANES), BF16),
            pltpu.VMEM((pairs, n_head * rows, LANES), BF16),
            pltpu.VMEM((n_z * CORES * rows, 2 * LANES), F32),
            pltpu.VMEM((n_z * CORES * rows, 2 * LANES), F32),
            pltpu.VMEM((2, 8, LANES), F32),
            pltpu.VMEM((X * CORES, 8, LANES), F32),
            pltpu.VMEM((n_z, 8, LANES), F32),
            dma((9,)),
            dma((2,)),
            dma((3,)),
            dma((3,)),
            dma((X * CORES,)),
            dma((X * CORES,)),
            dma((n_z,)),
            dma((n_z,)),
            dma((n_z, 2)),
            dma((n_z, 2)),
            dma((X, CORES)),
            dma((X, CORES)),
            dma((X, CORES)),
            dma((pairs, X)),
            dma((n_head,)),
            dma((n_head,)),
            dma((n_head,)),
            dma((n_head,)),
            dma((n_head, 2)),
            dma((n_head, 2)),
            pltpu.SemaphoreType.REGULAR((2, 3)),
            pltpu.SemaphoreType.REGULAR,
        ],
        compiler_params=pltpu.CompilerParams(
            collective_id=0, has_side_effects=True, vmem_limit_bytes=40 * 1024 * 1024
        ),
    )(*[pltpu.with_memory_space_constraint(operand, pltpu.HBM) for operand in operands])
    return jnp.transpose(mixed)


def solution(mesh):
    in_specs = (
        P(("cfg", "patch"), None),
        P(),
        P(),
        P(None, "head"),
        P(None, "head"),
        P(None, "head"),
        P("head", None),
        P(("cfg", "patch"), "head"),
        P(("cfg", "patch"), "head"),
    )
    return jax.shard_map(
        functools.partial(per_device, mesh.shape["patch"], mesh.shape["head"]),
        mesh=mesh,
        in_specs=in_specs,
        out_specs=P(("cfg", "patch"), "head"),
        check_vma=False,
    )
```
